32 devices in a mesh: group: 2 (over y), region: 4 (over z), probe: 4 (over x, core).
Axes of the slice: x: 2, y: 2, z: 4, core: 2. Of those that a mesh axis runs over, the one named last changes fastest.
Arguments:
- object_slices: float32 [4, 2, 512, 256], P('group', None, 'region', 'probe'), parts along dimension 0, may hold values from -4 to 4
- probe: float32 [4, 128, 128], P('group'), parts along dimension 0, may hold values from -6 to 6
- intensity: float32 [4, 16, 256, 128], P('region', 'probe', 'group'), parts along dimension 2, may hold values from 0.5 to 4
- positions: int32 [4, 16, 4], P('region', 'probe', 'group'), parts along dimension 2, may hold values from 0 to 255, as said below
Outputs:
- gradient: float32 [4, 2, 512, 256], P('group', None, 'region', 'probe'), parts along dimension 0
The draws below stay inside these ranges and needn't reach their ends.
There are 2 independent parts, one for each index of `group`. The reference program is written for one: setup_inputs(seed, part) draws one part's arguments, and reference() takes and returns one part's arrays. A program takes and returns all parts, laid end to end along the dimension named above; each array names one. Nothing has to cross between parts.
Inputs may be any that keep to these rules, and one draw needn't show every extreme that they name: `positions`: entry 0 is a row offset below 128 within the region's rows, entry 1 a column offset below 256.
All inputs are finite; a program needn't handle non-finite values.
Results may differ from the reference program's by a relative error of at most 0.00014.
Values sent between devices are 32-bit elements; how exact they have to be, the bound alone decides.
A program may use at most 64 MiB of HBM per device.

```python
import jax
import jax.numpy as jnp

WINDOW = 128
SLICES = 2
BAND = 128
REGIONS = 4
REGION_POS = 16
ROWS = 512
COLUMNS = 256


def draw_positions(key, part):
    first_key, second_key = jax.random.split(key)
    row_offsets = jax.random.randint(first_key, (REGIONS, REGION_POS), 0, BAND, dtype=jnp.int32)
    col_offsets = jax.random.randint(second_key, (REGIONS, REGION_POS), 0, COLUMNS, dtype=jnp.int32)
    stacked = jnp.stack([row_offsets, col_offsets], axis=-1)
    stacked = stacked.at[0, 0].set(jnp.array([BAND - 1, COLUMNS - 1], jnp.int32))
    stacked = stacked.at[0, 1].set(jnp.zeros((2,), jnp.int32))
    return stacked


def shard_levels(stream_key, shape, shards, smallest, high):
    def one(axis_at, blocks):
        heights = jax.random.uniform(jax.random.fold_in(jax.random.fold_in(stream_key, 6), axis_at), (blocks,), jnp.float32, smallest / len(shards), high / len(shards))
        return jnp.repeat(jnp.exp(heights), shape[axis_at] // blocks).reshape((-1,) + (1,) * (len(shape) - axis_at - 1))

    gain = one(*shards[0])
    for cut in shards[1:]:
        gain = gain * one(*cut)
    return gain


def scatter_about(rng, dims, spread, limit, shards=(), held_as=jnp.bfloat16):
    values = jax.random.normal(rng, dims, jnp.float32) * spread
    if len(shards) > 0:
        values = shard_levels(rng, dims, shards, -0.22, 0.18) * values
    return jnp.clip(values, min=-limit, max=limit).astype(held_as)


def setup_inputs(seed: int = 0, part: int = 0) -> dict:
    arg_keys = jax.random.split(jax.random.key(seed), 5)
    own_keys = jax.random.split(jax.random.fold_in(arg_keys[4], part), 5)
    object_slices = scatter_about(own_keys[0], (SLICES, 2, ROWS, COLUMNS), 0.7, 4.0, ((2, 4), (3, 4)), jnp.float32)
    probe = scatter_about(own_keys[1], (2, WINDOW, WINDOW), 1.0, 6.0, (), jnp.float32)
    intensity = jnp.clip(0.5 + 3.5 * jax.random.uniform(own_keys[2], (REGIONS, REGION_POS, WINDOW, WINDOW), jnp.float32) ** shard_levels(own_keys[2], (REGIONS, REGION_POS, WINDOW, WINDOW), ((0, 4), (1, 4)), -0.2, 0.2), 0.5, 4.0)
    positions = draw_positions(jax.random.fold_in(jax.random.fold_in(arg_keys[4], part), 71), part)
    return {"object_slices": object_slices, "probe": probe, "intensity": intensity, "positions": positions}


def propagator(window):
    indices = jnp.arange(window, dtype=jnp.int32)
    frequency = jnp.where(indices < window // 2, indices, indices - window).astype(jnp.float32) / window
    phases = -60.0 * (frequency[:, None] ** 2 + frequency[None, :] ** 2)
    return jnp.cos(phases), jnp.sin(phases)


def reference(object_slices, probe, intensity, positions):
    object_field = object_slices[:, 0] + 1j * object_slices[:, 1]
    probe_wave = probe[0] + 1j * probe[1]
    kernel_re, kernel_im = propagator(WINDOW)
    kernel = kernel_re + 1j * kernel_im
    offsets = jnp.arange(WINDOW, dtype=jnp.int32)
    gradient = jnp.zeros(object_field.shape, object_field.dtype)
    for region in range(REGIONS):
        row_index = (region * BAND + positions[region, :, 0][:, None] + offsets[None, :]) % ROWS
        col_index = (positions[region, :, 1][:, None] + offsets[None, :]) % COLUMNS
        patches = object_field[:, row_index[:, :, None], col_index[:, None, :]]
        incoming = jnp.broadcast_to(probe_wave, patches.shape[1:])
        waves_in = []
        exit_wave = incoming
        for layer in range(SLICES):
            waves_in.append(incoming)
            exit_wave = incoming * patches[layer]
            if layer < SLICES - 1:
                incoming = jnp.fft.ifft2(kernel * jnp.fft.fft2(exit_wave, norm="ortho"), norm="ortho")
        far_field = jnp.fft.fft2(exit_wave, norm="ortho")
        misfit = far_field.real ** 2 + far_field.imag ** 2 - intensity[region]
        returned = jnp.fft.ifft2(misfit * far_field, norm="ortho")
        layer_grads = [None] * SLICES
        for layer in reversed(range(SLICES)):
            layer_grads[layer] = jnp.conj(waves_in[layer]) * returned
            if layer > 0:
                moved = jnp.fft.fft2(jnp.conj(patches[layer]) * returned, norm="ortho")
                returned = jnp.fft.ifft2(jnp.conj(kernel) * moved, norm="ortho")
        gradient = gradient.at[:, row_index[:, :, None], col_index[:, None, :]].add(jnp.stack(layer_grads))
    gradient = gradient / REGION_POS
    return jnp.stack([gradient.real, gradient.imag], axis=1).astype(jnp.float32)
```

```python
import functools
import math

import jax
import jax.numpy as jnp
import ml_dtypes
import numpy as np
from jax import lax
from jax.experimental import pallas as pl
from jax.experimental.pallas import tpu as pltpu
from jax.sharding import PartitionSpec as P

MESH = pl.DeviceIdType.MESH
VMEM_BYTES = 48 * 1024 * 1024


def halves(matrix):
    high = matrix.astype(np.float32).astype(ml_dtypes.bfloat16)
    low = (matrix - high.astype(np.float64)).astype(np.float32).astype(ml_dtypes.bfloat16)
    return high, low


def tables(window):
    index = np.arange(window)
    angle = (index[:, None] * index[None, :] % window) * (2.0 * math.pi / window)
    re = np.cos(angle) / math.sqrt(window)
    im = -np.sin(angle) / math.sqrt(window)
    forward = np.block([[re, im], [-im, re]])
    high, low = halves(forward)
    high_t, low_t = halves(forward.T)
    frequency = np.where(index < window // 2, index, index - window) / window
    phase = -60.0 * (frequency[:, None] ** 2 + frequency[None, :] ** 2)
    mover = np.stack([np.cos(phase), np.sin(phase)]).astype(np.float32)
    return np.stack([high, low, high_t, low_t]), mover


def split(values):
    high = values.astype(jnp.bfloat16)
    low = (values - high.astype(jnp.float32)).astype(jnp.bfloat16)
    return high, low


def product(left, right):
    dot = functools.partial(jnp.dot, preferred_element_type=jnp.float32)
    return dot(left[0], right[0]) + (dot(left[1], right[0]) + dot(left[0], right[1]))


def kernel(
    sizes, pos_ref, obj_ref, probe_ref, intensity_ref, table_ref, mover_ref, out_ref,
    tiles, canvas, spread, give, take, total, final,
    tile_send, tile_recv, sum_send, sum_recv,
):
    layers, chips, regions, items, window = sizes
    columns = chips * window
    half = window // 2
    me = lax.axis_index("probe")
    band = lax.axis_index("region")
    chip = me // 2
    core = me % 2
    twin = {"probe": me + 1 - 2 * core, "region": band}
    places = [(b, d) for b in range(2) for d in range(chips)]
    first = core == 0
    lane = lax.broadcasted_iota(jnp.int32, (window, window), 1)
    in_left = lane < half

    def device(shift, band_shift):
        return {
            "probe": (chip + chips + shift) % chips * 2 + core,
            "region": (band + regions + band_shift) % regions,
        }

    barrier = pltpu.get_barrier_semaphore()
    peers = [twin] + [
        device(d, b) for d in range(chips) for b in (0, -1, 1) if (d, b) != (0, 0)
    ]
    for peer in peers:
        pl.semaphore_signal(barrier, inc=1, device_id=peer, device_id_type=MESH)
    for layer in range(layers):
        tiles[layer, 0, 0, 0] = jnp.concatenate([obj_ref[layer, 0], obj_ref[layer, 1]], axis=1)
    margin = jnp.zeros((window, window), jnp.float32)
    for n in range(items):
        for plane in range(2):
            for d in range(chips):
                spread[n, plane, d, 0:window] = margin
                spread[n, plane, d, 2 * window : 3 * window] = margin
    pl.semaphore_wait(barrier, len(peers))

    def tile_copy(layer, b, d):
        return pltpu.make_async_remote_copy(
            src_ref=tiles.at[layer, 0, 0, 0],
            dst_ref=tiles.at[layer, b, d, 0],
            send_sem=tile_send.at[layer, b, d, 0],
            recv_sem=tile_recv.at[layer, b, d, 0],
            device_id=device(-d, -b),
            device_id_type=MESH,
        )

    def tile_pass(layer, b, d):
        return pltpu.make_async_remote_copy(
            src_ref=tiles.at[layer, b, d, 0],
            dst_ref=tiles.at[layer, b, d, 1],
            send_sem=tile_send.at[layer, b, d, 1],
            recv_sem=tile_recv.at[layer, b, d, 1],
            device_id=twin,
            device_id_type=MESH,
        )

    def sum_pass(layer, b, d):
        return pltpu.make_async_remote_copy(
            src_ref=give.at[layer, b, d],
            dst_ref=take.at[layer, b, d],
            send_sem=sum_send.at[layer, b, d, 0],
            recv_sem=sum_recv.at[layer, b, d, 0],
            device_id=twin,
            device_id_type=MESH,
        )

    def sum_copy(layer, b, d):
        return pltpu.make_async_remote_copy(
            src_ref=total.at[layer, b, d],
            dst_ref=final.at[layer, b, d],
            send_sem=sum_send.at[layer, b, d, 1],
            recv_sem=sum_recv.at[layer, b, d, 1],
            device_id=device(d, b),
            device_id_type=MESH,
        )

    away = places[1:]
    for layer in range(layers):
        for b, d in away:
            tile_copy(layer, b, d).start()
        tile_pass(layer, 0, 0).start()

    def relay(layer):
        for b, d in away:
            tile_copy(layer, b, d).wait_recv()
            tile_pass(layer, b, d).start()

    def assemble(layer):
        for b, d in places:
            tile_pass(layer, b, d).wait_recv()
            same, other = tiles[layer, b, d, 0], tiles[layer, b, d, 1]
            west = jnp.where(first, same, other)
            east = jnp.where(first, other, same)
            rows = slice(b * window, (b + 1) * window)
            canvas[layer, 0, d, rows] = jnp.where(in_left, west, pltpu.roll(east, half, 1))
            canvas[layer, 1, d, rows] = jnp.where(in_left, pltpu.roll(west, half, 1), east)

    row = [pos_ref[0, n, 0] for n in range(items)]
    col = [(pos_ref[0, n, 1] + columns - chip * window) % columns for n in range(items)]

    def cut(layer):
        patches = []
        for n in range(items):
            both = []
            for plane in range(2):
                strip = jnp.concatenate(
                    [canvas[layer, plane, d, pl.ds(row[n], window), :] for d in range(chips)],
                    axis=1,
                )
                both.append(pltpu.roll(strip, (columns - col[n]) % columns, 1)[:, :window])
            patches.append(tuple(both))
        return patches

    def on_rows(waves, which):
        stacked = jnp.concatenate([jnp.concatenate(w, axis=1) for w in waves], axis=0)
        matrix = (table_ref[2 * which], table_ref[2 * which + 1])
        out = product(split(stacked), matrix)
        return [
            (out[n * window : (n + 1) * window, :window], out[n * window : (n + 1) * window, window:])
            for n in range(len(waves))
        ]

    def on_columns(waves, which):
        stacked = jnp.concatenate([jnp.concatenate(w, axis=0) for w in waves], axis=1)
        matrix = (table_ref[2 - 2 * which], table_ref[3 - 2 * which])
        out = product(matrix, split(stacked))
        return [
            (out[:window, n * window : (n + 1) * window], out[window:, n * window : (n + 1) * window])
            for n in range(len(waves))
        ]

    def forward(waves):
        return on_rows(on_columns(waves, 0), 0)

    def backward(waves):
        return on_columns(on_rows(waves, 1), 1)

    def times(a, b):
        return (a[0] * b[0] - a[1] * b[1], a[0] * b[1] + a[1] * b[0])

    def conj_times(a, b):
        return (a[0] * b[0] + a[1] * b[1], a[0] * b[1] - a[1] * b[0])

    mover = (mover_ref[0], mover_ref[1])

    def scatter(layer, grads):
        blank = jnp.zeros((window, columns - window), jnp.float32)
        for n in range(items):
            for plane in range(2):
                wide = jnp.concatenate([grads[n][plane], blank], axis=1)
                wide = pltpu.roll(wide, col[n], 1)
                for d in range(chips):
                    spread[n, plane, d, window : 2 * window] = wide[:, d * window : (d + 1) * window]
        for b, d in places:
            re, im = [
                sum(
                    spread[n, plane, d, pl.ds((b + 1) * window - row[n], window), :]
                    for n in range(items)
                )
                for plane in range(2)
            ]
            west = jnp.where(in_left, re, pltpu.roll(im, half, 1))
            east = jnp.where(in_left, pltpu.roll(re, half, 1), im)
            total[layer, b, d] = jnp.where(first, west, east)
            give[layer, b, d] = jnp.where(first, east, west)
            sum_pass(layer, b, d).start()

    def share(layer):
        for b, d in away + places[:1]:
            sum_pass(layer, b, d).wait_recv()
            total[layer, b, d] = total[layer, b, d] + take[layer, b, d]
            if (b, d) != (0, 0):
                sum_copy(layer, b, d).start()

    relay(0)
    assemble(0)
    incident = [[(probe_ref[0], probe_ref[1])] * items]
    patches = []
    for layer in range(layers):
        patches.append(cut(layer))
        leaving = [times(w, p) for w, p in zip(incident[layer], patches[layer])]
        far = forward(leaving)
        if layer < layers - 1:
            relay(layer + 1)
            incident.append(backward([times(mover, w) for w in far]))
            assemble(layer + 1)
    residual = []
    for n in range(items):
        re, im = far[n]
        misfit = re * re + im * im - intensity_ref[0, n]
        residual.append((misfit * re, misfit * im))
    back = backward(residual)
    for layer in reversed(range(layers)):
        scatter(layer, [conj_times(w, g) for w, g in zip(incident[layer], back)])
        if layer > 0:
            far = forward([conj_times(p, g) for p, g in zip(patches[layer], back)])
            share(layer)
            back = backward([conj_times(mover, w) for w in far])
    share(0)
    scale = 1.0 / (items * 2 * chips)
    for layer in reversed(range(layers)):
        value = total[layer, 0, 0]
        for b, d in away:
            sum_copy(layer, b, d).wait_recv()
            value = value + final[layer, b, d]
        value = value * scale
        out_ref[layer, 0] = value[:, :half]
        out_ref[layer, 1] = value[:, half:]
    for layer in range(layers):
        for b, d in places:
            tile_pass(layer, b, d).wait_send()
            sum_pass(layer, b, d).wait_send()
        for b, d in away:
            tile_copy(layer, b, d).wait_send()
            sum_copy(layer, b, d).wait_send()


def body(object_slices, probe, intensity, positions):
    layers = object_slices.shape[0]
    window = probe.shape[1]
    items = positions.shape[1]
    chips = lax.axis_size("probe") // 2
    regions = lax.axis_size("region")
    table, mover = tables(window)
    f32 = jnp.float32
    whole = pl.BlockSpec(memory_space=pltpu.VMEM)
    return pl.pallas_call(
        functools.partial(kernel, (layers, chips, regions, items, window)),
        out_shape=jax.ShapeDtypeStruct(object_slices.shape, f32),
        in_specs=[pl.BlockSpec(memory_space=pltpu.SMEM)] + [whole] * 5,
        out_specs=whole,
        scratch_shapes=[
            pltpu.VMEM((layers, 2, chips, 2, window, window), f32),
            pltpu.VMEM((layers, 2, chips, 2 * window, window), f32),
            pltpu.VMEM((items, 2, chips, 3 * window, window), f32),
            pltpu.VMEM((layers, 2, chips, window, window), f32),
            pltpu.VMEM((layers, 2, chips, window, window), f32),
            pltpu.VMEM((layers, 2, chips, window, window), f32),
            pltpu.VMEM((layers, 2, chips, window, window), f32),
        ]
        + [pltpu.SemaphoreType.DMA((layers, 2, chips, 2))] * 4,
        compiler_params=pltpu.CompilerParams(
            collective_id=0, has_side_effects=True, vmem_limit_bytes=VMEM_BYTES
        ),
    )(positions, object_slices, probe, intensity, jnp.asarray(table), jnp.asarray(mover))


def solution(mesh):
    placed = (
        P("group", None, "region", "probe"),
        P("group", None, None),
        P("region", "probe", "group", None),
        P("region", "probe", "group"),
    )
    return jax.shard_map(
        body,
        mesh=mesh,
        in_specs=placed,
        out_specs=P("group", None, "region", "probe"),
        check_vma=False,
    )
```

```python
import functools
import math

import jax
import jax.numpy as jnp
import ml_dtypes
import numpy as np
from jax import lax
from jax.experimental import pallas as pl
from jax.experimental.pallas import tpu as pltpu
from jax.sharding import PartitionSpec as P

MESH = pl.DeviceIdType.MESH
VMEM_BYTES = 48 * 1024 * 1024


def halves(matrix):
    high = matrix.astype(np.float32).astype(ml_dtypes.bfloat16)
    low = (matrix - high.astype(np.float64)).astype(np.float32).astype(ml_dtypes.bfloat16)
    return high, low


def tables(window):
    index = np.arange(window)
    angle = (index[:, None] * index[None, :] % window) * (2.0 * math.pi / window)
    re = np.cos(angle) / math.sqrt(window)
    im = -np.sin(angle) / math.sqrt(window)
    forward = np.block([[re, im], [-im, re]])
    high, low = halves(forward)
    frequency = np.where(index < window // 2, index, index - window) / window
    phase = -60.0 * (frequency[:, None] ** 2 + frequency[None, :] ** 2)
    mover = np.stack([np.cos(phase), np.sin(phase)]).astype(np.float32)
    return np.stack([high, low]), mover


def split(values):
    high = values.astype(jnp.bfloat16)
    low = (values - high.astype(jnp.float32)).astype(jnp.bfloat16)
    return high, low


def product(left, right):
    wide = jnp.concatenate([left[0], left[1], left[0]], axis=1)
    tall = jnp.concatenate([right[0], right[0], right[1]], axis=0)
    return jnp.dot(wide, tall, preferred_element_type=jnp.float32)


def kernel(
    sizes, pos_ref, obj_ref, probe_hbm, intensity_hbm, table_hbm, mover_hbm, out_ref,
    probe_ref, intensity_ref, table_ref, mover_ref, load_sem,
    tiles, canvas, spread, give, take, total, final,
    tile_send, tile_recv, sum_send, sum_recv,
):
    layers, chips, regions, items, window = sizes
    columns = chips * window
    half = window // 2
    me = lax.axis_index("probe")
    band = lax.axis_index("region")
    chip = me // 2
    core = me % 2
    twin = {"probe": me + 1 - 2 * core, "region": band}
    places = [(b, d) for b in range(2) for d in range(chips)]
    first = core == 0
    lane = lax.broadcasted_iota(jnp.int32, (window, window), 1)
    in_left = lane < half

    def device(shift, band_shift):
        return {
            "probe": (chip + chips + shift) % chips * 2 + core,
            "region": (band + regions + band_shift) % regions,
        }

    barrier = pltpu.get_barrier_semaphore()
    peers = [twin] + [
        device(d, b) for d in range(chips) for b in (0, -1, 1) if (d, b) != (0, 0)
    ]
    for peer in peers:
        pl.semaphore_signal(barrier, inc=1, device_id=peer, device_id_type=MESH)
    loads = [
        pltpu.make_async_copy(source, target, load_sem.at[i])
        for i, (source, target) in enumerate(
            [
                (probe_hbm, probe_ref),
                (table_hbm, table_ref),
                (mover_hbm, mover_ref),
                (intensity_hbm, intensity_ref),
            ]
        )
    ]
    for load in loads:
        load.start()
    for layer in range(layers):
        both = jnp.concatenate([obj_ref[layer, 0], obj_ref[layer, 1]], axis=0)
        tiles[layer, 0, 0, 0] = both.T
    margin = jnp.zeros((window, window), jnp.float32)
    for n in range(items):
        for plane in range(2):
            for d in range(chips):
                spread[n, plane, d, 0:window] = margin
                spread[n, plane, d, 2 * window : 3 * window] = margin
    pl.semaphore_wait(barrier, len(peers))

    def tile_copy(layer, b, d):
        return pltpu.make_async_remote_copy(
            src_ref=tiles.at[layer, 0, 0, 0],
            dst_ref=tiles.at[layer, b, d, 0],
            send_sem=tile_send.at[layer, b, d, 0],
            recv_sem=tile_recv.at[layer, b, d, 0],
            device_id=device(-d, -b),
            device_id_type=MESH,
        )

    def tile_pass(layer, b, d):
        return pltpu.make_async_remote_copy(
            src_ref=tiles.at[layer, b, d, 0],
            dst_ref=tiles.at[layer, b, d, 1],
            send_sem=tile_send.at[layer, b, d, 1],
            recv_sem=tile_recv.at[layer, b, d, 1],
            device_id=twin,
            device_id_type=MESH,
        )

    def sum_pass(layer, b, d):
        return pltpu.make_async_remote_copy(
            src_ref=give.at[layer, b, d],
            dst_ref=take.at[layer, b, d],
            send_sem=sum_send.at[layer, b, d, 0],
            recv_sem=sum_recv.at[layer, b, d, 0],
            device_id=twin,
            device_id_type=MESH,
        )

    def sum_copy(layer, b, d):
        return pltpu.make_async_remote_copy(
            src_ref=total.at[layer, b, d],
            dst_ref=final.at[layer, b, d],
            send_sem=sum_send.at[layer, b, d, 1],
            recv_sem=sum_recv.at[layer, b, d, 1],
            device_id=device(d, b),
            device_id_type=MESH,
        )

    away = places[1:]
    for layer in range(layers):
        for b, d in away[::-1]:
            tile_copy(layer, b, d).start()
        tile_pass(layer, 0, 0).start()

    def relay(layer):
        for b, d in away:
            tile_copy(layer, b, d).wait_recv()
            tile_pass(layer, b, d).start()

    def assemble(layer):
        for b, d in places:
            tile_pass(layer, b, d).wait_recv()
            same, other = tiles[layer, b, d, 0], tiles[layer, b, d, 1]
            west = jnp.where(first, same, other)
            east = jnp.where(first, other, same)
            rows = slice(b * window, (b + 1) * window)
            canvas[layer, 0, d, rows] = jnp.where(in_left, west, pltpu.roll(east, half, 1))
            canvas[layer, 1, d, rows] = jnp.where(in_left, pltpu.roll(west, half, 1), east)

    row = [pos_ref[0, 0, n] for n in range(items)]
    col = [(pos_ref[0, 1, n] + columns - chip * window) % columns for n in range(items)]

    def cut(layer):
        patches = []
        for n in range(items):
            both = []
            for plane in range(2):
                strip = jnp.concatenate(
                    [canvas[layer, plane, d, pl.ds(row[n], window), :] for d in range(chips)],
                    axis=1,
                )
                both.append(pltpu.roll(strip, (columns - col[n]) % columns, 1)[:, :window])
            patches.append(tuple(both))
        return patches

    def on_rows(waves):
        stacked = jnp.concatenate([jnp.concatenate(w, axis=1) for w in waves], axis=0)
        out = product(split(stacked), (table_ref[0], table_ref[1]))
        return [
            (out[n * window : (n + 1) * window, :window], out[n * window : (n + 1) * window, window:])
            for n in range(len(waves))
        ]

    def on_columns(waves):
        stacked = jnp.concatenate([jnp.concatenate(w, axis=0) for w in waves], axis=1)
        out = product((table_ref[0], table_ref[1]), split(stacked))
        return [
            (out[:window, n * window : (n + 1) * window], out[window:, n * window : (n + 1) * window])
            for n in range(len(waves))
        ]

    def swap(waves):
        return [(w[1], w[0]) for w in waves]

    def forward(waves):
        return on_rows(swap(on_columns(swap(waves))))

    def backward(waves):
        return on_columns(swap(on_rows(swap(waves))))

    def times(a, b):
        return (a[0] * b[0] - a[1] * b[1], a[0] * b[1] + a[1] * b[0])

    def conj_times(a, b):
        return (a[0] * b[0] + a[1] * b[1], a[0] * b[1] - a[1] * b[0])

    def scatter(layer, grads):
        blank = jnp.zeros((window, columns - window), jnp.float32)
        for n in range(items):
            for plane in range(2):
                wide = jnp.concatenate([grads[n][plane], blank], axis=1)
                wide = pltpu.roll(wide, col[n], 1)
                for d in range(chips):
                    spread[n, plane, d, window : 2 * window] = wide[:, d * window : (d + 1) * window]
        for b, d in away[::-1] + places[:1]:
            re, im = [
                sum(
                    spread[n, plane, d, pl.ds((b + 1) * window - row[n], window), :]
                    for n in range(items)
                )
                for plane in range(2)
            ]
            west = jnp.where(in_left, re, pltpu.roll(im, half, 1))
            east = jnp.where(in_left, pltpu.roll(re, half, 1), im)
            total[layer, b, d] = jnp.where(first, west, east)
            give[layer, b, d] = jnp.where(first, east, west)
            sum_pass(layer, b, d).start()

    def share(layer):
        for b, d in away[::-1] + places[:1]:
            sum_pass(layer, b, d).wait_recv()
            total[layer, b, d] = total[layer, b, d] + take[layer, b, d]
            if (b, d) != (0, 0):
                sum_copy(layer, b, d).start()

    relay(0)
    for load in loads:
        load.wait()
    mover = (mover_ref[0], mover_ref[1])
    assemble(0)
    incident = [[(probe_ref[0], probe_ref[1])] * items]
    patches = []
    for layer in range(layers):
        patches.append(cut(layer))
        leaving = [times(w, p) for w, p in zip(incident[layer], patches[layer])]
        far = forward(leaving)
        if layer < layers - 1:
            relay(layer + 1)
            incident.append(backward([times(mover, w) for w in far]))
            assemble(layer + 1)
    residual = []
    for n in range(items):
        re, im = far[n]
        misfit = re * re + im * im - intensity_ref[0, n]
        residual.append((misfit * re, misfit * im))
    back = backward(residual)
    for layer in reversed(range(layers)):
        scatter(layer, [conj_times(w, g) for w, g in zip(incident[layer], back)])
        if layer > 0:
            far = forward([conj_times(p, g) for p, g in zip(patches[layer], back)])
            share(layer)
            back = backward([conj_times(mover, w) for w in far])
    share(0)
    scale = 1.0 / (items * 2 * chips)
    for layer in reversed(range(layers)):
        value = total[layer, 0, 0]
        for b, d in away:
            sum_copy(layer, b, d).wait_recv()
            value = value + final[layer, b, d]
        value = value * scale
        value = value.T
        out_ref[layer, 0] = value[:half]
        out_ref[layer, 1] = value[half:]
    for layer in range(layers):
        for b, d in places:
            tile_pass(layer, b, d).wait_send()
            sum_pass(layer, b, d).wait_send()
        for b, d in away:
            tile_copy(layer, b, d).wait_send()
            sum_copy(layer, b, d).wait_send()


def body(object_slices, probe, intensity, positions):
    layers = object_slices.shape[0]
    window = probe.shape[1]
    items = positions.shape[1]
    chips = lax.axis_size("probe") // 2
    regions = lax.axis_size("region")
    table, mover = tables(window)
    f32 = jnp.float32
    whole = pl.BlockSpec(memory_space=pltpu.VMEM)
    kept = pl.BlockSpec(memory_space=pltpu.HBM)
    turned = object_slices.transpose(0, 1, 3, 2)
    result = pl.pallas_call(
        functools.partial(kernel, (layers, chips, regions, items, window)),
        out_shape=jax.ShapeDtypeStruct(turned.shape, f32),
        in_specs=[pl.BlockSpec(memory_space=pltpu.SMEM), whole] + [kept] * 4,
        out_specs=whole,
        scratch_shapes=[
            pltpu.VMEM(probe.shape, f32),
            pltpu.VMEM(intensity.shape, f32),
            pltpu.VMEM(table.shape, jnp.bfloat16),
            pltpu.VMEM(mover.shape, f32),
            pltpu.SemaphoreType.DMA((4,)),
            pltpu.VMEM((layers, 2, chips, 2, window, window), f32),
            pltpu.VMEM((layers, 2, chips, 2 * window, window), f32),
            pltpu.VMEM((items, 2, chips, 3 * window, window), f32),
            pltpu.VMEM((layers, 2, chips, window, window), f32),
            pltpu.VMEM((layers, 2, chips, window, window), f32),
            pltpu.VMEM((layers, 2, chips, window, window), f32),
            pltpu.VMEM((layers, 2, chips, window, window), f32),
        ]
        + [pltpu.SemaphoreType.DMA((layers, 2, chips, 2))] * 4,
        compiler_params=pltpu.CompilerParams(
            collective_id=0, has_side_effects=True, vmem_limit_bytes=VMEM_BYTES
        ),
    )(positions.transpose(0, 2, 1), turned, probe, intensity, jnp.asarray(table), jnp.asarray(mover))
    return result.transpose(0, 1, 3, 2)


def solution(mesh):
    placed = (
        P("group", None, "region", "probe"),
        P("group", None, None),
        P("region", "probe", "group", None),
        P("region", "probe", "group"),
    )
    return jax.shard_map(
        body,
        mesh=mesh,
        in_specs=placed,
        out_specs=P("group", None, "region", "probe"),
        check_vma=False,
    )
```

```python
import functools
import math

import jax
import jax.numpy as jnp
import ml_dtypes
import numpy as np
from jax import lax
from jax.experimental import pallas as pl
from jax.experimental.pallas import tpu as pltpu
from jax.sharding import PartitionSpec as P

MESH = pl.DeviceIdType.MESH
VMEM_BYTES = 48 * 1024 * 1024


def halves(matrix):
    high = matrix.astype(np.float32).astype(ml_dtypes.bfloat16)
    low = (matrix - high.astype(np.float64)).astype(np.float32).astype(ml_dtypes.bfloat16)
    return high, low


def tables(window):
    index = np.arange(window)
    angle = (index[:, None] * index[None, :] % window) * (2.0 * math.pi / window)
    re = np.cos(angle) / math.sqrt(window)
    im = -np.sin(angle) / math.sqrt(window)
    forward = np.block([[re, im], [-im, re]])
    high, low = halves(forward)
    frequency = np.where(index < window // 2, index, index - window) / window
    phase = -60.0 * (frequency[:, None] ** 2 + frequency[None, :] ** 2)
    mover = np.stack([np.cos(phase), np.sin(phase)]).astype(np.float32)
    return np.stack([high, low]), mover


def split(values):
    high = values.astype(jnp.bfloat16)
    low = (values - high.astype(jnp.float32)).astype(jnp.bfloat16)
    return high, low


def product(left, right):
    wide = jnp.concatenate([left[0], left[1], left[0]], axis=1)
    tall = jnp.concatenate([right[0], right[0], right[1]], axis=0)
    return jnp.dot(wide, tall, preferred_element_type=jnp.float32)


def kernel(
    sizes, pos_ref, obj_ref, probe_hbm, intensity_hbm, table_hbm, mover_hbm, out_ref,
    probe_ref, intensity_ref, table_ref, mover_ref, load_sem,
    tiles, canvas, spread, give, take, total, final,
    tile_send, tile_recv, sum_send, sum_recv,
):
    layers, chips, regions, items, window = sizes
    columns = chips * window
    half = window // 2
    me = lax.axis_index("probe")
    band = lax.axis_index("region")
    chip = me // 2
    core = me % 2
    twin = {"probe": me + 1 - 2 * core, "region": band}
    places = [(b, d) for b in range(2) for d in range(chips)]
    first = core == 0
    lane = lax.broadcasted_iota(jnp.int32, (window, window), 1)
    in_left = lane < half

    def device(shift, band_shift):
        return {
            "probe": (chip + chips + shift) % chips * 2 + core,
            "region": (band + regions + band_shift) % regions,
        }

    barrier = pltpu.get_barrier_semaphore()
    peers = [twin] + [
        device(d, b) for d in range(chips) for b in (0, -1, 1) if (d, b) != (0, 0)
    ]
    for peer in peers:
        pl.semaphore_signal(barrier, inc=1, device_id=peer, device_id_type=MESH)
    loads = [
        pltpu.make_async_copy(source, target, load_sem.at[i])
        for i, (source, target) in enumerate(
            [
                (probe_hbm, probe_ref),
                (table_hbm, table_ref),
                (mover_hbm, mover_ref),
                (intensity_hbm, intensity_ref),
            ]
        )
    ]
    for load in loads:
        load.start()
    for layer in range(layers):
        both = jnp.concatenate([obj_ref[layer, 0], obj_ref[layer, 1]], axis=0)
        tiles[layer, 0, 0, 0] = both.T
    margin = jnp.zeros((window, window), jnp.float32)
    for n in range(items):
        for plane in range(2):
            for d in range(chips):
                spread[n, plane, d, 0:window] = margin
                spread[n, plane, d, 2 * window : 3 * window] = margin
    pl.semaphore_wait(barrier, len(peers))

    def tile_copy(layer, b, d):
        return pltpu.make_async_remote_copy(
            src_ref=tiles.at[layer, 0, 0, 0],
            dst_ref=tiles.at[layer, b, d, 0],
            send_sem=tile_send.at[layer, b, d, 0],
            recv_sem=tile_recv.at[layer, b, d, 0],
            device_id=device(-d, -b),
            device_id_type=MESH,
        )

    def tile_pass(layer, b, d):
        return pltpu.make_async_remote_copy(
            src_ref=tiles.at[layer, b, d, 0],
            dst_ref=tiles.at[layer, b, d, 1],
            send_sem=tile_send.at[layer, b, d, 1],
            recv_sem=tile_recv.at[layer, b, d, 1],
            device_id=twin,
            device_id_type=MESH,
        )

    def sum_pass(layer, b, d):
        return pltpu.make_async_remote_copy(
            src_ref=give.at[layer, b, d],
            dst_ref=take.at[layer, b, d],
            send_sem=sum_send.at[layer, b, d, 0],
            recv_sem=sum_recv.at[layer, b, d, 0],
            device_id=twin,
            device_id_type=MESH,
        )

    def sum_copy(layer, b, d):
        return pltpu.make_async_remote_copy(
            src_ref=total.at[layer, b, d],
            dst_ref=final.at[layer, b, d],
            send_sem=sum_send.at[layer, b, d, 1],
            recv_sem=sum_recv.at[layer, b, d, 1],
            device_id=device(d, b),
            device_id_type=MESH,
        )

    away = places[1:]
    for layer in range(layers):
        for b, d in away[::-1]:
            tile_copy(layer, b, d).start()
        tile_pass(layer, 0, 0).start()

    def relay(layer):
        for b, d in away:
            tile_copy(layer, b, d).wait_recv()
            tile_pass(layer, b, d).start()

    def assemble(layer):
        for b, d in places:
            tile_pass(layer, b, d).wait_recv()
            same, other = tiles[layer, b, d, 0], tiles[layer, b, d, 1]
            west = jnp.where(first, same, other)
            east = jnp.where(first, other, same)
            rows = slice(b * window, (b + 1) * window)
            canvas[layer, 0, d, rows] = jnp.where(in_left, west, pltpu.roll(east, half, 1))
            canvas[layer, 1, d, rows] = jnp.where(in_left, pltpu.roll(west, half, 1), east)

    row = [pos_ref[0, 0, n] for n in range(items)]
    col = [(pos_ref[0, 1, n] + columns - chip * window) % columns for n in range(items)]

    def cut(layer):
        patches = []
        for n in range(items):
            both = []
            for plane in range(2):
                strip = jnp.concatenate(
                    [canvas[layer, plane, d, pl.ds(row[n], window), :] for d in range(chips)],
                    axis=1,
                )
                both.append(pltpu.roll(strip, (columns - col[n]) % columns, 1)[:, :window])
            patches.append(tuple(both))
        return patches

    def on_rows(waves):
        stacked = jnp.concatenate([jnp.concatenate(w, axis=1) for w in waves], axis=0)
        out = product(split(stacked), (table_ref[0], table_ref[1]))
        return [
            (out[n * window : (n + 1) * window, :window], out[n * window : (n + 1) * window, window:])
            for n in range(len(waves))
        ]

    def on_columns(waves):
        stacked = jnp.concatenate([jnp.concatenate(w, axis=0) for w in waves], axis=1)
        out = product((table_ref[0], table_ref[1]), split(stacked))
        return [
            (out[:window, n * window : (n + 1) * window], out[window:, n * window : (n + 1) * window])
            for n in range(len(waves))
        ]

    def swap(waves):
        return [(w[1], w[0]) for w in waves]

    def forward(waves):
        return on_rows(swap(on_columns(swap(waves))))

    def backward(waves):
        return on_columns(swap(on_rows(swap(waves))))

    def times(a, b):
        return (a[0] * b[0] - a[1] * b[1], a[0] * b[1] + a[1] * b[0])

    def conj_times(a, b):
        return (a[0] * b[0] + a[1] * b[1], a[0] * b[1] - a[1] * b[0])

    def scatter(layer, grads):
        blank = jnp.zeros((window, columns - window), jnp.float32)
        for n in range(items):
            for plane in range(2):
                wide = jnp.concatenate([grads[n][plane], blank], axis=1)
                wide = pltpu.roll(wide, col[n], 1)
                for d in range(chips):
                    spread[n, plane, d, window : 2 * window] = wide[:, d * window : (d + 1) * window]
        for b, d in away[::-1] + places[:1]:
            re, im = [
                sum(
                    spread[n, plane, d, pl.ds((b + 1) * window - row[n], window), :]
                    for n in range(items)
                )
                for plane in range(2)
            ]
            west = jnp.where(in_left, re, pltpu.roll(im, half, 1))
            east = jnp.where(in_left, pltpu.roll(re, half, 1), im)
            total[layer, b, d] = jnp.where(first, west, east)
            give[layer, b, d] = jnp.where(first, east, west)
            sum_pass(layer, b, d).start()

    def share(layer):
        for b, d in away[::-1] + places[:1]:
            sum_pass(layer, b, d).wait_recv()
            total[layer, b, d] = total[layer, b, d] + take[layer, b, d]
            if (b, d) != (0, 0):
                sum_copy(layer, b, d).start()

    relay(0)
    for load in loads:
        load.wait()
    mover = (mover_ref[0], mover_ref[1])
    assemble(0)
    incident = [[(probe_ref[0], probe_ref[1])] * items]
    patches = []
    for layer in range(layers):
        patches.append(cut(layer))
        leaving = [times(w, p) for w, p in zip(incident[layer], patches[layer])]
        far = forward(leaving)
        if layer < layers - 1:
            relay(layer + 1)
            incident.append(backward([times(mover, w) for w in far]))
            assemble(layer + 1)
    residual = []
    for n in range(items):
        re, im = far[n]
        misfit = re * re + im * im - intensity_ref[0, n]
        residual.append((misfit * re, misfit * im))
    back = backward(residual)
    for layer in reversed(range(layers)):
        scatter(layer, [conj_times(w, g) for w, g in zip(incident[layer], back)])
        if layer > 0:
            far = forward([conj_times(p, g) for p, g in zip(patches[layer], back)])
            share(layer)
            back = backward([conj_times(mover, w) for w in far])
    share(0)
    scale = 1.0 / (items * 2 * chips)
    for layer in reversed(range(layers)):
        value = total[layer, 0, 0]
        for b, d in away:
            sum_copy(layer, b, d).wait_recv()
            value = value + final[layer, b, d]
        value = value * scale
        value = value.T
        out_ref[layer, 0] = value[:half]
        out_ref[layer, 1] = value[half:]
    for layer in range(layers):
        for b, d in places:
            tile_pass(layer, b, d).wait_send()
            sum_pass(layer, b, d).wait_send()
        for b, d in away:
            tile_copy(layer, b, d).wait_send()
            sum_copy(layer, b, d).wait_send()


def body(object_slices, probe, intensity, positions):
    layers = object_slices.shape[0]
    window = probe.shape[1]
    items = positions.shape[1]
    chips = lax.axis_size("probe") // 2
    regions = lax.axis_size("region")
    table, mover = tables(window)
    f32 = jnp.float32
    whole = pl.BlockSpec(memory_space=pltpu.VMEM)
    kept = pl.BlockSpec(memory_space=pl.ANY)
    turned = object_slices.transpose(0, 1, 3, 2)
    result = pl.pallas_call(
        functools.partial(kernel, (layers, chips, regions, items, window)),
        out_shape=jax.ShapeDtypeStruct(turned.shape, f32),
        in_specs=[pl.BlockSpec(memory_space=pltpu.SMEM), whole] + [kept] * 4,
        out_specs=whole,
        scratch_shapes=[
            pltpu.VMEM(probe.shape, f32),
            pltpu.VMEM(intensity.shape, f32),
            pltpu.VMEM(table.shape, jnp.bfloat16),
            pltpu.VMEM(mover.shape, f32),
            pltpu.SemaphoreType.DMA((4,)),
            pltpu.VMEM((layers, 2, chips, 2, window, window), f32),
            pltpu.VMEM((layers, 2, chips, 2 * window, window), f32),
            pltpu.VMEM((items, 2, chips, 3 * window, window), f32),
            pltpu.VMEM((layers, 2, chips, window, window), f32),
            pltpu.VMEM((layers, 2, chips, window, window), f32),
            pltpu.VMEM((layers, 2, chips, window, window), f32),
            pltpu.VMEM((layers, 2, chips, window, window), f32),
        ]
        + [pltpu.SemaphoreType.DMA((layers, 2, chips, 2))] * 4,
        compiler_params=pltpu.CompilerParams(
            collective_id=0, has_side_effects=True, vmem_limit_bytes=VMEM_BYTES
        ),
    )(positions.transpose(0, 2, 1), turned, probe, intensity, jnp.asarray(table), jnp.asarray(mover))
    return result.transpose(0, 1, 3, 2)


def solution(mesh):
    placed = (
        P("group", None, "region", "probe"),
        P("group", None, None),
        P("region", "probe", "group", None),
        P("region", "probe", "group"),
    )
    return jax.shard_map(
        body,
        mesh=mesh,
        in_specs=placed,
        out_specs=P("group", None, "region", "probe"),
        check_vma=False,
    )
```

```python
import functools
import math

import jax
import jax.numpy as jnp
import ml_dtypes
import numpy as np
from jax import lax
from jax.experimental import pallas as pl
from jax.experimental.pallas import tpu as pltpu
from jax.sharding import PartitionSpec as P

MESH = pl.DeviceIdType.MESH
VMEM_BYTES = 48 * 1024 * 1024


def halves(matrix):
    high = matrix.astype(np.float32).astype(ml_dtypes.bfloat16)
    low = (matrix - high.astype(np.float64)).astype(np.float32).astype(ml_dtypes.bfloat16)
    return high, low


def tables(window):
    index = np.arange(window)
    angle = (index[:, None] * index[None, :] % window) * (2.0 * math.pi / window)
    dft = np.exp(-1j * angle) / math.sqrt(window)
    frequency = np.where(index < window // 2, index, index - window) / window
    move = dft.conj() @ (np.exp(-60j * frequency**2)[:, None] * dft)
    parts = []
    for matrix in (dft, move):
        parts += halves(np.block([[matrix.real, matrix.imag], [-matrix.imag, matrix.real]]))
    return np.stack(parts)


def split(values):
    high = values.astype(jnp.bfloat16)
    low = (values - high.astype(jnp.float32)).astype(jnp.bfloat16)
    return high, low


def product(left, right):
    wide = jnp.concatenate([left[0], left[1], left[0]], axis=1)
    tall = jnp.concatenate([right[0], right[0], right[1]], axis=0)
    return jnp.dot(wide, tall, preferred_element_type=jnp.float32)


def kernel(
    sizes, pos_ref, obj_ref, probe_ref, intensity_ref, table_ref, out_ref,
    tiles, canvas, spread, give, take, total, final,
    tile_send, tile_recv, sum_send, sum_recv,
):
    layers, chips, regions, items, window = sizes
    columns = chips * window
    half = window // 2
    me = lax.axis_index("probe")
    band = lax.axis_index("region")
    chip = me // 2
    core = me % 2
    twin = {"probe": me + 1 - 2 * core, "region": band}
    places = [(b, d) for b in range(2) for d in range(chips)]
    first = core == 0
    lane = lax.broadcasted_iota(jnp.int32, (window, window), 1)
    in_left = lane < half

    def device(shift, band_shift):
        return {
            "probe": (chip + chips + shift) % chips * 2 + core,
            "region": (band + regions + band_shift) % regions,
        }

    barrier = pltpu.get_barrier_semaphore()
    peers = [twin] + [
        device(d, b) for d in range(chips) for b in (0, -1, 1) if (d, b) != (0, 0)
    ]
    for peer in peers:
        pl.semaphore_signal(barrier, inc=1, device_id=peer, device_id_type=MESH)
    for layer in range(layers):
        tiles[layer, 0, 0, 0] = jnp.concatenate([obj_ref[layer, 0], obj_ref[layer, 1]], axis=1)
    margin = jnp.zeros((window, window), jnp.float32)
    for n in range(items):
        for plane in range(2):
            for d in range(chips):
                spread[n, plane, d, 0:window] = margin
                spread[n, plane, d, 2 * window : 3 * window] = margin
    pl.semaphore_wait(barrier, len(peers))

    def tile_copy(layer, b, d):
        return pltpu.make_async_remote_copy(
            src_ref=tiles.at[layer, 0, 0, 0],
            dst_ref=tiles.at[layer, b, d, 0],
            send_sem=tile_send.at[layer, b, d, 0],
            recv_sem=tile_recv.at[layer, b, d, 0],
            device_id=device(-d, -b),
            device_id_type=MESH,
        )

    def tile_pass(layer, b, d):
        return pltpu.make_async_remote_copy(
            src_ref=tiles.at[layer, b, d, 0],
            dst_ref=tiles.at[layer, b, d, 1],
            send_sem=tile_send.at[layer, b, d, 1],
            recv_sem=tile_recv.at[layer, b, d, 1],
            device_id=twin,
            device_id_type=MESH,
        )

    def sum_pass(layer, b, d):
        return pltpu.make_async_remote_copy(
            src_ref=give.at[layer, b, d],
            dst_ref=take.at[layer, b, d],
            send_sem=sum_send.at[layer, b, d, 0],
            recv_sem=sum_recv.at[layer, b, d, 0],
            device_id=twin,
            device_id_type=MESH,
        )

    def sum_copy(layer, b, d):
        return pltpu.make_async_remote_copy(
            src_ref=total.at[layer, b, d],
            dst_ref=final.at[layer, b, d],
            send_sem=sum_send.at[layer, b, d, 1],
            recv_sem=sum_recv.at[layer, b, d, 1],
            device_id=device(d, b),
            device_id_type=MESH,
        )

    away = places[1:]
    for layer in range(layers):
        for b, d in away:
            tile_copy(layer, b, d).start()
        tile_pass(layer, 0, 0).start()

    def relay(layer):
        for b, d in away:
            tile_copy(layer, b, d).wait_recv()
            tile_pass(layer, b, d).start()

    def assemble(layer):
        for b, d in places:
            tile_pass(layer, b, d).wait_recv()
            same, other = tiles[layer, b, d, 0], tiles[layer, b, d, 1]
            west = jnp.where(first, same, other)
            east = jnp.where(first, other, same)
            rows = slice(b * window, (b + 1) * window)
            canvas[layer, 0, d, rows] = jnp.where(in_left, west, pltpu.roll(east, half, 1))
            canvas[layer, 1, d, rows] = jnp.where(in_left, pltpu.roll(west, half, 1), east)

    row = [pos_ref[0, n, 0] for n in range(items)]
    col = [(pos_ref[0, n, 1] + columns - chip * window) % columns for n in range(items)]

    def cut(layer):
        patches = []
        for n in range(items):
            both = []
            for plane in range(2):
                strip = jnp.concatenate(
                    [canvas[layer, plane, d, pl.ds(row[n], window), :] for d in range(chips)],
                    axis=1,
                )
                both.append(pltpu.roll(strip, (columns - col[n]) % columns, 1)[:, :window])
            patches.append(tuple(both))
        return patches

    def on_rows(waves, which):
        stacked = jnp.concatenate([jnp.concatenate(w, axis=1) for w in waves], axis=0)
        matrix = (table_ref[2 * which], table_ref[2 * which + 1])
        out = product(split(stacked), matrix)
        return [
            (out[n * window : (n + 1) * window, :window], out[n * window : (n + 1) * window, window:])
            for n in range(len(waves))
        ]

    def on_columns(waves, which):
        stacked = jnp.concatenate([jnp.concatenate(w, axis=0) for w in waves], axis=1)
        matrix = (table_ref[2 * which], table_ref[2 * which + 1])
        out = product(matrix, split(stacked))
        return [
            (out[:window, n * window : (n + 1) * window], out[window:, n * window : (n + 1) * window])
            for n in range(len(waves))
        ]

    def swap(waves):
        return [(w[1], w[0]) for w in waves]

    def nothing():
        pass

    def forward(waves, which, between=nothing):
        waves = swap(on_columns(swap(waves), which))
        between()
        return on_rows(waves, which)

    def backward(waves, which, between=nothing):
        waves = swap(on_rows(swap(waves), which))
        between()
        return on_columns(waves, which)

    def times(a, b):
        return (a[0] * b[0] - a[1] * b[1], a[0] * b[1] + a[1] * b[0])

    def conj_times(a, b):
        return (a[0] * b[0] + a[1] * b[1], a[0] * b[1] - a[1] * b[0])

    def scatter(layer, grads):
        blank = jnp.zeros((window, columns - window), jnp.float32)
        for n in range(items):
            for plane in range(2):
                wide = jnp.concatenate([grads[n][plane], blank], axis=1)
                wide = pltpu.roll(wide, col[n], 1)
                for d in range(chips):
                    spread[n, plane, d, window : 2 * window] = wide[:, d * window : (d + 1) * window]
        for b, d in away[::-1] + places[:1]:
            re, im = [
                sum(
                    spread[n, plane, d, pl.ds((b + 1) * window - row[n], window), :]
                    for n in range(items)
                )
                for plane in range(2)
            ]
            west = jnp.where(in_left, re, pltpu.roll(im, half, 1))
            east = jnp.where(in_left, pltpu.roll(re, half, 1), im)
            total[layer, b, d] = jnp.where(first, west, east)
            give[layer, b, d] = jnp.where(first, east, west)
            sum_pass(layer, b, d).start()

    def share(layer):
        for b, d in away[::-1] + places[:1]:
            sum_pass(layer, b, d).wait_recv()
            total[layer, b, d] = total[layer, b, d] + take[layer, b, d]
            if (b, d) != (0, 0):
                sum_copy(layer, b, d).start()

    relay(0)
    assemble(0)
    incident = [[(probe_ref[0], probe_ref[1])] * items]
    patches = []
    for layer in range(layers):
        patches.append(cut(layer))
        leaving = [times(w, p) for w, p in zip(incident[layer], patches[layer])]
        if layer < layers - 1:
            incident.append(forward(leaving, 1, functools.partial(relay, layer + 1)))
            assemble(layer + 1)
    far = forward(leaving, 0)
    residual = []
    for n in range(items):
        re, im = far[n]
        misfit = re * re + im * im - intensity_ref[0, n]
        residual.append((misfit * re, misfit * im))
    back = backward(residual, 0)
    for layer in reversed(range(layers)):
        scatter(layer, [conj_times(w, g) for w, g in zip(incident[layer], back)])
        if layer > 0:
            carried = [conj_times(p, g) for p, g in zip(patches[layer], back)]
            back = backward(carried, 1, functools.partial(share, layer))
    share(0)
    scale = 1.0 / (items * 2 * chips)
    for layer in reversed(range(layers)):
        value = total[layer, 0, 0]
        for b, d in away:
            sum_copy(layer, b, d).wait_recv()
            value = value + final[layer, b, d]
        value = value * scale
        out_ref[layer, 0] = value[:, :half]
        out_ref[layer, 1] = value[:, half:]
    for layer in range(layers):
        for b, d in places:
            tile_pass(layer, b, d).wait_send()
            sum_pass(layer, b, d).wait_send()
        for b, d in away:
            tile_copy(layer, b, d).wait_send()
            sum_copy(layer, b, d).wait_send()


def body(object_slices, probe, intensity, positions):
    layers = object_slices.shape[0]
    window = probe.shape[1]
    items = positions.shape[1]
    chips = lax.axis_size("probe") // 2
    regions = lax.axis_size("region")
    table = tables(window)
    f32 = jnp.float32
    whole = pl.BlockSpec(memory_space=pltpu.VMEM)
    return pl.pallas_call(
        functools.partial(kernel, (layers, chips, regions, items, window)),
        out_shape=jax.ShapeDtypeStruct(object_slices.shape, f32),
        in_specs=[pl.BlockSpec(memory_space=pltpu.SMEM)] + [whole] * 4,
        out_specs=whole,
        scratch_shapes=[
            pltpu.VMEM((layers, 2, chips, 2, window, window), f32),
            pltpu.VMEM((layers, 2, chips, 2 * window, window), f32),
            pltpu.VMEM((items, 2, chips, 3 * window, window), f32),
            pltpu.VMEM((layers, 2, chips, window, window), f32),
            pltpu.VMEM((layers, 2, chips, window, window), f32),
            pltpu.VMEM((layers, 2, chips, window, window), f32),
            pltpu.VMEM((layers, 2, chips, window, window), f32),
        ]
        + [pltpu.SemaphoreType.DMA((layers, 2, chips, 2))] * 4,
        compiler_params=pltpu.CompilerParams(
            collective_id=0, has_side_effects=True, vmem_limit_bytes=VMEM_BYTES
        ),
    )(positions, object_slices, probe, intensity, jnp.asarray(table))


def solution(mesh):
    placed = (
        P("group", None, "region", "probe"),
        P("group", None, None),
        P("region", "probe", "group", None),
        P("region", "probe", "group"),
    )
    return jax.shard_map(
        body,
        mesh=mesh,
        in_specs=placed,
        out_specs=P("group", None, "region", "probe"),
        check_vma=False,
    )
```

```python
import functools
import math

import jax
import jax.numpy as jnp
import ml_dtypes
import numpy as np
from jax import lax
from jax.experimental import pallas as pl
from jax.experimental.pallas import tpu as pltpu
from jax.sharding import PartitionSpec as P

MESH = pl.DeviceIdType.MESH
VMEM_BYTES = 48 * 1024 * 1024


def halves(matrix):
    high = matrix.astype(np.float32).astype(ml_dtypes.bfloat16)
    low = (matrix - high.astype(np.float64)).astype(np.float32).astype(ml_dtypes.bfloat16)
    return high, low


def tables(window):
    index = np.arange(window)
    angle = (index[:, None] * index[None, :] % window) * (2.0 * math.pi / window)
    dft = np.exp(-1j * angle) / math.sqrt(window)
    frequency = np.where(index < window // 2, index, index - window) / window
    move = dft.conj() @ (np.exp(-60j * frequency**2)[:, None] * dft)
    parts = []
    for matrix in (dft, move):
        parts += halves(np.block([[matrix.real, matrix.imag], [-matrix.imag, matrix.real]]))
    return np.stack(parts)


def split(values):
    high = values.astype(jnp.bfloat16)
    low = (values - high.astype(jnp.float32)).astype(jnp.bfloat16)
    return high, low


def product(left, right):
    wide = jnp.concatenate([left[0], left[1], left[0]], axis=1)
    tall = jnp.concatenate([right[0], right[0], right[1]], axis=0)
    return jnp.dot(wide, tall, preferred_element_type=jnp.float32)


def kernel(
    sizes, pos_ref, obj_ref, probe_ref, intensity_ref, table_ref, out_ref,
    tiles, canvas, spread, give, take, total, final,
    tile_send, tile_recv, sum_send, sum_recv,
):
    layers, chips, regions, items, window = sizes
    columns = chips * window
    half = window // 2
    me = lax.axis_index("probe")
    band = lax.axis_index("region")
    chip = me // 2
    core = me % 2
    twin = {"probe": me + 1 - 2 * core, "region": band}
    places = [(b, d) for b in range(2) for d in range(chips)]
    first = core == 0
    lane = lax.broadcasted_iota(jnp.int32, (window, window), 1)
    in_left = lane < half

    def device(shift, band_shift):
        return {
            "probe": (chip + chips + shift) % chips * 2 + core,
            "region": (band + regions + band_shift) % regions,
        }

    barrier = pltpu.get_barrier_semaphore()
    peers = [twin] + [
        device(d, b) for d in range(chips) for b in (0, -1, 1) if (d, b) != (0, 0)
    ]
    for peer in peers:
        pl.semaphore_signal(barrier, inc=1, device_id=peer, device_id_type=MESH)
    for layer in range(layers):
        tiles[layer, 0, 0, 0] = jnp.concatenate([obj_ref[layer, 0], obj_ref[layer, 1]], axis=1)
    margin = jnp.zeros((window, window), jnp.float32)
    for n in range(items):
        for plane in range(2):
            for d in range(chips):
                spread[n, plane, d, 0:window] = margin
                spread[n, plane, d, 2 * window : 3 * window] = margin
    pl.semaphore_wait(barrier, len(peers))

    def tile_copy(layer, b, d):
        return pltpu.make_async_remote_copy(
            src_ref=tiles.at[layer, 0, 0, 0],
            dst_ref=tiles.at[layer, b, d, 0],
            send_sem=tile_send.at[layer, b, d, 0],
            recv_sem=tile_recv.at[layer, b, d, 0],
            device_id=device(-d, -b),
            device_id_type=MESH,
        )

    def tile_pass(layer, b, d):
        return pltpu.make_async_remote_copy(
            src_ref=tiles.at[layer, b, d, 0],
            dst_ref=tiles.at[layer, b, d, 1],
            send_sem=tile_send.at[layer, b, d, 1],
            recv_sem=tile_recv.at[layer, b, d, 1],
            device_id=twin,
            device_id_type=MESH,
        )

    def sum_pass(layer, b, d):
        return pltpu.make_async_remote_copy(
            src_ref=give.at[layer, b, d],
            dst_ref=take.at[layer, b, d],
            send_sem=sum_send.at[layer, b, d, 0],
            recv_sem=sum_recv.at[layer, b, d, 0],
            device_id=twin,
            device_id_type=MESH,
        )

    def sum_copy(layer, b, d):
        return pltpu.make_async_remote_copy(
            src_ref=total.at[layer, b, d],
            dst_ref=final.at[layer, b, d],
            send_sem=sum_send.at[layer, b, d, 1],
            recv_sem=sum_recv.at[layer, b, d, 1],
            device_id=device(d, b),
            device_id_type=MESH,
        )

    away = places[1:]

    def launch(layer):
        for b, d in away[::-1]:
            tile_copy(layer, b, d).start()
        tile_pass(layer, 0, 0).start()

    def relay(layer):
        for b, d in away:
            tile_copy(layer, b, d).wait_recv()
            tile_pass(layer, b, d).start()
        if layer < layers - 1:
            launch(layer + 1)

    def assemble(layer):
        for b, d in places:
            tile_pass(layer, b, d).wait_recv()
            same, other = tiles[layer, b, d, 0], tiles[layer, b, d, 1]
            west = jnp.where(first, same, other)
            east = jnp.where(first, other, same)
            rows = slice(b * window, (b + 1) * window)
            canvas[layer, 0, d, rows] = jnp.where(in_left, west, pltpu.roll(east, half, 1))
            canvas[layer, 1, d, rows] = jnp.where(in_left, pltpu.roll(west, half, 1), east)

    row = [pos_ref[0, n, 0] for n in range(items)]
    col = [(pos_ref[0, n, 1] + columns - chip * window) % columns for n in range(items)]

    def cut(layer):
        patches = []
        for n in range(items):
            both = []
            for plane in range(2):
                strip = jnp.concatenate(
                    [canvas[layer, plane, d, pl.ds(row[n], window), :] for d in range(chips)],
                    axis=1,
                )
                both.append(pltpu.roll(strip, (columns - col[n]) % columns, 1)[:, :window])
            patches.append(tuple(both))
        return patches

    def on_rows(waves, which):
        stacked = jnp.concatenate([jnp.concatenate(w, axis=1) for w in waves], axis=0)
        matrix = (table_ref[2 * which], table_ref[2 * which + 1])
        out = product(split(stacked), matrix)
        return [
            (out[n * window : (n + 1) * window, :window], out[n * window : (n + 1) * window, window:])
            for n in range(len(waves))
        ]

    def on_columns(waves, which):
        stacked = jnp.concatenate([jnp.concatenate(w, axis=0) for w in waves], axis=1)
        matrix = (table_ref[2 * which], table_ref[2 * which + 1])
        out = product(matrix, split(stacked))
        return [
            (out[:window, n * window : (n + 1) * window], out[window:, n * window : (n + 1) * window])
            for n in range(len(waves))
        ]

    def swap(waves):
        return [(w[1], w[0]) for w in waves]

    def nothing():
        pass

    def forward(waves, which, between=nothing):
        waves = swap(on_columns(swap(waves), which))
        between()
        return on_rows(waves, which)

    def backward(waves, which, between=nothing):
        waves = swap(on_rows(swap(waves), which))
        between()
        return on_columns(waves, which)

    def times(a, b):
        return (a[0] * b[0] - a[1] * b[1], a[0] * b[1] + a[1] * b[0])

    def conj_times(a, b):
        return (a[0] * b[0] + a[1] * b[1], a[0] * b[1] - a[1] * b[0])

    def scatter(layer, grads):
        blank = jnp.zeros((window, columns - window), jnp.float32)
        for n in range(items):
            for plane in range(2):
                wide = jnp.concatenate([grads[n][plane], blank], axis=1)
                wide = pltpu.roll(wide, col[n], 1)
                for d in range(chips):
                    spread[n, plane, d, window : 2 * window] = wide[:, d * window : (d + 1) * window]
        for b, d in away[::-1] + places[:1]:
            re, im = [
                sum(
                    spread[n, plane, d, pl.ds((b + 1) * window - row[n], window), :]
                    for n in range(items)
                )
                for plane in range(2)
            ]
            west = jnp.where(in_left, re, pltpu.roll(im, half, 1))
            east = jnp.where(in_left, pltpu.roll(re, half, 1), im)
            total[layer, b, d] = jnp.where(first, west, east)
            give[layer, b, d] = jnp.where(first, east, west)
            sum_pass(layer, b, d).start()

    def share(layer):
        for b, d in away[::-1] + places[:1]:
            sum_pass(layer, b, d).wait_recv()
            total[layer, b, d] = total[layer, b, d] + take[layer, b, d]
            if (b, d) != (0, 0):
                sum_copy(layer, b, d).start()

    launch(0)
    relay(0)
    assemble(0)
    incident = [[(probe_ref[0], probe_ref[1])] * items]
    patches = []
    for layer in range(layers):
        patches.append(cut(layer))
        leaving = [times(w, p) for w, p in zip(incident[layer], patches[layer])]
        if layer < layers - 1:
            incident.append(forward(leaving, 1, functools.partial(relay, layer + 1)))
            assemble(layer + 1)
    far = forward(leaving, 0)
    residual = []
    for n in range(items):
        re, im = far[n]
        misfit = re * re + im * im - intensity_ref[0, n]
        residual.append((misfit * re, misfit * im))
    back = backward(residual, 0)
    for layer in reversed(range(layers)):
        scatter(layer, [conj_times(w, g) for w, g in zip(incident[layer], back)])
        if layer > 0:
            carried = [conj_times(p, g) for p, g in zip(patches[layer], back)]
            back = backward(carried, 1, functools.partial(share, layer))
    share(0)
    scale = 1.0 / (items * 2 * chips)
    for layer in reversed(range(layers)):
        value = total[layer, 0, 0]
        for b, d in away:
            sum_copy(layer, b, d).wait_recv()
            value = value + final[layer, b, d]
        value = value * scale
        out_ref[layer, 0] = value[:, :half]
        out_ref[layer, 1] = value[:, half:]
    for layer in range(layers):
        for b, d in places:
            tile_pass(layer, b, d).wait_send()
            sum_pass(layer, b, d).wait_send()
        for b, d in away:
            tile_copy(layer, b, d).wait_send()
            sum_copy(layer, b, d).wait_send()


def body(object_slices, probe, intensity, positions):
    layers = object_slices.shape[0]
    window = probe.shape[1]
    items = positions.shape[1]
    chips = lax.axis_size("probe") // 2
    regions = lax.axis_size("region")
    table = tables(window)
    f32 = jnp.float32
    whole = pl.BlockSpec(memory_space=pltpu.VMEM)
    return pl.pallas_call(
        functools.partial(kernel, (layers, chips, regions, items, window)),
        out_shape=jax.ShapeDtypeStruct(object_slices.shape, f32),
        in_specs=[pl.BlockSpec(memory_space=pltpu.SMEM)] + [whole] * 4,
        out_specs=whole,
        scratch_shapes=[
            pltpu.VMEM((layers, 2, chips, 2, window, window), f32),
            pltpu.VMEM((layers, 2, chips, 2 * window, window), f32),
            pltpu.VMEM((items, 2, chips, 3 * window, window), f32),
            pltpu.VMEM((layers, 2, chips, window, window), f32),
            pltpu.VMEM((layers, 2, chips, window, window), f32),
            pltpu.VMEM((layers, 2, chips, window, window), f32),
            pltpu.VMEM((layers, 2, chips, window, window), f32),
        ]
        + [pltpu.SemaphoreType.DMA((layers, 2, chips, 2))] * 4,
        compiler_params=pltpu.CompilerParams(
            collective_id=0, has_side_effects=True, vmem_limit_bytes=VMEM_BYTES
        ),
    )(positions, object_slices, probe, intensity, jnp.asarray(table))


def solution(mesh):
    placed = (
        P("group", None, "region", "probe"),
        P("group", None, None),
        P("region", "probe", "group", None),
        P("region", "probe", "group"),
    )
    return jax.shard_map(
        body,
        mesh=mesh,
        in_specs=placed,
        out_specs=P("group", None, "region", "probe"),
        check_vma=False,
    )
```

```python
import functools
import math

import jax
import jax.numpy as jnp
import ml_dtypes
import numpy as np
from jax import lax
from jax.experimental import pallas as pl
from jax.experimental.pallas import tpu as pltpu
from jax.sharding import PartitionSpec as P

MESH = pl.DeviceIdType.MESH
VMEM_BYTES = 48 * 1024 * 1024


def halves(matrix):
    high = matrix.astype(np.float32).astype(ml_dtypes.bfloat16)
    low = (matrix - high.astype(np.float64)).astype(np.float32).astype(ml_dtypes.bfloat16)
    return high, low


def tables(window):
    index = np.arange(window)
    angle = (index[:, None] * index[None, :] % window) * (2.0 * math.pi / window)
    dft = np.exp(-1j * angle) / math.sqrt(window)
    frequency = np.where(index < window // 2, index, index - window) / window
    move = dft.conj() @ (np.exp(-60j * frequency**2)[:, None] * dft)
    parts = []
    for matrix in (dft, move):
        parts += halves(np.block([[matrix.real, matrix.imag], [-matrix.imag, matrix.real]]))
    return np.stack(parts)


def split(values):
    high = values.astype(jnp.bfloat16)
    low = (values - high.astype(jnp.float32)).astype(jnp.bfloat16)
    return high, low


def product(left, right):
    wide = jnp.concatenate([left[0], left[1], left[0]], axis=1)
    tall = jnp.concatenate([right[0], right[0], right[1]], axis=0)
    return jnp.dot(wide, tall, preferred_element_type=jnp.float32)


def kernel(
    sizes, pos_ref, obj_ref, probe_ref, intensity_ref, table_ref, out_ref,
    tiles, canvas, spread, give, take, total, final,
    tile_send, tile_recv, sum_send, sum_recv,
):
    layers, chips, regions, items, window = sizes
    columns = chips * window
    half = window // 2
    me = lax.axis_index("probe")
    band = lax.axis_index("region")
    chip = me // 2
    core = me % 2
    twin = {"probe": me + 1 - 2 * core, "region": band}
    places = [(b, d) for b in range(2) for d in range(chips)]
    first = core == 0
    lane = lax.broadcasted_iota(jnp.int32, (window, window), 1)
    in_left = lane < half

    def device(shift, band_shift):
        return {
            "probe": (chip + chips + shift) % chips * 2 + core,
            "region": (band + regions + band_shift) % regions,
        }

    barrier = pltpu.get_barrier_semaphore()
    peers = [twin] + [
        device(d, b) for d in range(chips) for b in (0, -1, 1) if (d, b) != (0, 0)
    ]
    for peer in peers:
        pl.semaphore_signal(barrier, inc=1, device_id=peer, device_id_type=MESH)
    for layer in range(layers):
        tiles[layer, 0, 0, 0] = jnp.concatenate([obj_ref[layer, 0], obj_ref[layer, 1]], axis=1)
    margin = jnp.zeros((window, window), jnp.float32)
    for n in range(items):
        for plane in range(2):
            for d in range(chips):
                spread[n, plane, d, 0:window] = margin
                spread[n, plane, d, 2 * window : 3 * window] = margin
    pl.semaphore_wait(barrier, len(peers))

    def tile_copy(layer, b, d):
        return pltpu.make_async_remote_copy(
            src_ref=tiles.at[layer, 0, 0, 0],
            dst_ref=tiles.at[layer, b, d, 0],
            send_sem=tile_send.at[layer, b, d, 0],
            recv_sem=tile_recv.at[layer, b, d, 0],
            device_id=device(-d, -b),
            device_id_type=MESH,
        )

    def tile_pass(layer, b, d):
        return pltpu.make_async_remote_copy(
            src_ref=tiles.at[layer, b, d, 0],
            dst_ref=tiles.at[layer, b, d, 1],
            send_sem=tile_send.at[layer, b, d, 1],
            recv_sem=tile_recv.at[layer, b, d, 1],
            device_id=twin,
            device_id_type=MESH,
        )

    def sum_pass(layer, b, d):
        return pltpu.make_async_remote_copy(
            src_ref=give.at[layer, b, d],
            dst_ref=take.at[layer, b, d],
            send_sem=sum_send.at[layer, b, d, 0],
            recv_sem=sum_recv.at[layer, b, d, 0],
            device_id=twin,
            device_id_type=MESH,
        )

    def sum_copy(layer, b, d):
        return pltpu.make_async_remote_copy(
            src_ref=total.at[layer, b, d],
            dst_ref=final.at[layer, b, d],
            send_sem=sum_send.at[layer, b, d, 1],
            recv_sem=sum_recv.at[layer, b, d, 1],
            device_id=device(d, b),
            device_id_type=MESH,
        )

    away = places[1:]
    for layer in range(layers):
        for b, d in away:
            tile_copy(layer, b, d).start()
        tile_pass(layer, 0, 0).start()

    def relay(layer):
        for b, d in away:
            tile_copy(layer, b, d).wait_recv()
            tile_pass(layer, b, d).start()

    def assemble(layer):
        for b, d in places:
            tile_pass(layer, b, d).wait_recv()
            same, other = tiles[layer, b, d, 0], tiles[layer, b, d, 1]
            west = jnp.where(first, same, other)
            east = jnp.where(first, other, same)
            rows = slice(b * window, (b + 1) * window)
            canvas[layer, 0, d, rows] = jnp.where(in_left, west, pltpu.roll(east, half, 1))
            canvas[layer, 1, d, rows] = jnp.where(in_left, pltpu.roll(west, half, 1), east)

    row = [pos_ref[0, n, 0] for n in range(items)]
    col = [(pos_ref[0, n, 1] + columns - chip * window) % columns for n in range(items)]

    def cut(layer):
        patches = []
        for n in range(items):
            both = []
            for plane in range(2):
                strip = jnp.concatenate(
                    [canvas[layer, plane, d, pl.ds(row[n], window), :] for d in range(chips)],
                    axis=1,
                )
                both.append(pltpu.roll(strip, (columns - col[n]) % columns, 1)[:, :window])
            patches.append(tuple(both))
        return patches

    def on_rows(waves, which):
        if len(waves) > 2:
            return on_rows(waves[:2], which) + on_rows(waves[2:], which)
        stacked = jnp.concatenate([jnp.concatenate(w, axis=1) for w in waves], axis=0)
        matrix = (table_ref[2 * which], table_ref[2 * which + 1])
        out = product(split(stacked), matrix)
        return [
            (out[n * window : (n + 1) * window, :window], out[n * window : (n + 1) * window, window:])
            for n in range(len(waves))
        ]

    def on_columns(waves, which):
        if len(waves) > 2:
            return on_columns(waves[:2], which) + on_columns(waves[2:], which)
        stacked = jnp.concatenate([jnp.concatenate(w, axis=0) for w in waves], axis=1)
        matrix = (table_ref[2 * which], table_ref[2 * which + 1])
        out = product(matrix, split(stacked))
        return [
            (out[:window, n * window : (n + 1) * window], out[window:, n * window : (n + 1) * window])
            for n in range(len(waves))
        ]

    def swap(waves):
        return [(w[1], w[0]) for w in waves]

    def nothing():
        pass

    def forward(waves, which, between=nothing):
        waves = swap(on_columns(swap(waves), which))
        between()
        return on_rows(waves, which)

    def backward(waves, which, between=nothing):
        waves = swap(on_rows(swap(waves), which))
        between()
        return on_columns(waves, which)

    def times(a, b):
        return (a[0] * b[0] - a[1] * b[1], a[0] * b[1] + a[1] * b[0])

    def conj_times(a, b):
        return (a[0] * b[0] + a[1] * b[1], a[0] * b[1] - a[1] * b[0])

    def scatter(layer, grads):
        blank = jnp.zeros((window, columns - window), jnp.float32)
        for n in range(items):
            for plane in range(2):
                wide = jnp.concatenate([grads[n][plane], blank], axis=1)
                wide = pltpu.roll(wide, col[n], 1)
                for d in range(chips):
                    spread[n, plane, d, window : 2 * window] = wide[:, d * window : (d + 1) * window]
        for b, d in away[::-1] + places[:1]:
            re, im = [
                sum(
                    spread[n, plane, d, pl.ds((b + 1) * window - row[n], window), :]
                    for n in range(items)
                )
                for plane in range(2)
            ]
            west = jnp.where(in_left, re, pltpu.roll(im, half, 1))
            east = jnp.where(in_left, pltpu.roll(re, half, 1), im)
            total[layer, b, d] = jnp.where(first, west, east)
            give[layer, b, d] = jnp.where(first, east, west)
            sum_pass(layer, b, d).start()

    def share(layer):
        for b, d in away[::-1] + places[:1]:
            sum_pass(layer, b, d).wait_recv()
            total[layer, b, d] = total[layer, b, d] + take[layer, b, d]
            if (b, d) != (0, 0):
                sum_copy(layer, b, d).start()

    relay(0)
    assemble(0)
    incident = [[(probe_ref[0], probe_ref[1])] * items]
    patches = []
    for layer in range(layers):
        patches.append(cut(layer))
        leaving = [times(w, p) for w, p in zip(incident[layer], patches[layer])]
        if layer < layers - 1:
            incident.append(forward(leaving, 1, functools.partial(relay, layer + 1)))
            assemble(layer + 1)
    far = forward(leaving, 0)
    residual = []
    for n in range(items):
        re, im = far[n]
        misfit = re * re + im * im - intensity_ref[0, n]
        residual.append((misfit * re, misfit * im))
    back = backward(residual, 0)
    for layer in reversed(range(layers)):
        scatter(layer, [conj_times(w, g) for w, g in zip(incident[layer], back)])
        if layer > 0:
            carried = [conj_times(p, g) for p, g in zip(patches[layer], back)]
            back = backward(carried, 1, functools.partial(share, layer))
    share(0)
    scale = 1.0 / (items * 2 * chips)
    for layer in reversed(range(layers)):
        value = total[layer, 0, 0]
        for b, d in away:
            sum_copy(layer, b, d).wait_recv()
            value = value + final[layer, b, d]
        value = value * scale
        out_ref[layer, 0] = value[:, :half]
        out_ref[layer, 1] = value[:, half:]
    for layer in range(layers):
        for b, d in places:
            tile_pass(layer, b, d).wait_send()
            sum_pass(layer, b, d).wait_send()
        for b, d in away:
            tile_copy(layer, b, d).wait_send()
            sum_copy(layer, b, d).wait_send()


def body(object_slices, probe, intensity, positions):
    layers = object_slices.shape[0]
    window = probe.shape[1]
    items = positions.shape[1]
    chips = lax.axis_size("probe") // 2
    regions = lax.axis_size("region")
    table = tables(window)
    f32 = jnp.float32
    whole = pl.BlockSpec(memory_space=pltpu.VMEM)
    return pl.pallas_call(
        functools.partial(kernel, (layers, chips, regions, items, window)),
        out_shape=jax.ShapeDtypeStruct(object_slices.shape, f32),
        in_specs=[pl.BlockSpec(memory_space=pltpu.SMEM)] + [whole] * 4,
        out_specs=whole,
        scratch_shapes=[
            pltpu.VMEM((layers, 2, chips, 2, window, window), f32),
            pltpu.VMEM((layers, 2, chips, 2 * window, window), f32),
            pltpu.VMEM((items, 2, chips, 3 * window, window), f32),
            pltpu.VMEM((layers, 2, chips, window, window), f32),
            pltpu.VMEM((layers, 2, chips, window, window), f32),
            pltpu.VMEM((layers, 2, chips, window, window), f32),
            pltpu.VMEM((layers, 2, chips, window, window), f32),
        ]
        + [pltpu.SemaphoreType.DMA((layers, 2, chips, 2))] * 4,
        compiler_params=pltpu.CompilerParams(
            collective_id=0, has_side_effects=True, vmem_limit_bytes=VMEM_BYTES
        ),
    )(positions, object_slices, probe, intensity, jnp.asarray(table))


def solution(mesh):
    placed = (
        P("group", None, "region", "probe"),
        P("group", None, None),
        P("region", "probe", "group", None),
        P("region", "probe", "group"),
    )
    return jax.shard_map(
        body,
        mesh=mesh,
        in_specs=placed,
        out_specs=P("group", None, "region", "probe"),
        check_vma=False,
    )
```
